512 devices in a mesh: row: 32 (over z_hi, x, core), col: 16 (over z_lo, y).
Axes of the slice: x: 4, y: 4, z: 16 (z_hi: 4, z_lo: 4; z = z_hi * 4 + z_lo), core: 2. Of those that a mesh axis runs over, the one named last changes fastest.
Arguments:
- tiles: float32 [32, 16, 4, 512, 512], P('row', 'col'), may hold values from 0 to 16777212, as said below
- tile_index: int32 [32, 16, 4, 2], P('row', 'col'), may hold values from 0 to 15, as said below
- tile_count: int32 [32, 16], P('row', 'col'), may hold values from 0 to 4, as said below
- iterate: float32 [131072, 32], P(('row', 'col')), may hold values from 0 to 16777212, as said below
- basis: float32 [131072, 32], P(('row', 'col')), may hold values from 0 to 16777212, as said below
- coefficients: float32 [4096, 32, 32], P(('row', 'col')), may hold values from 0 to 16777212, as said below
- start_degree: int32 [1], replicated, may hold values from 1 to 4095
Outputs:
- scaled_iterate: float32 [131072, 32], P(('row', 'col'))
The draws below stay inside these ranges and needn't reach their ends.
Inputs may be any that keep to these rules, and one draw needn't show every extreme that they name: `tiles`: integers 0 to 16777212. `iterate`: integers 0 to 16777212. `basis`: integers 0 to 16777212. `coefficients`: integers 0 to 16777212. tile_index[..., 0] lies in 0 to 7 and tile_index[..., 1] in 0 to 15; the 4 slots of one device name distinct tiles, unoccupied slots included; unoccupied slots hold arbitrary entries. `tile_count`: some device has 4 occupied slots.
All inputs are finite; a program needn't handle non-finite values.
Results may differ from the reference program's by a relative error of at most 0.0003.
Values sent between devices are 32-bit elements; how exact they have to be, the bound alone decides.
No kernel may reach another device: no remote copies, remote signals or barrier semaphores. Data moves between devices by JAX's collectives and lax.ppermute only.
A program may use at most 64 MiB of HBM per device.

```python
import jax
import jax.numpy as jnp
from jax import lax

BW = 32
TILE = 512
ROWS_DEV = 256
TD = 4
STEPS = 2
ORDER = 131072
TR = 8
TC = 16
DEG = 4096
N_ROW = 32
N_COL = 16


def draw_residues(key, shape):
    return jax.random.randint(key, shape, 0, 16777213).astype(jnp.float32)


def layout_pick(key):
    pick_key = jax.random.fold_in(key, 21)
    block_key, tile_key, column_key = jax.random.split(pick_key, 3)
    empty_col = jax.random.randint(column_key, (), 0, TC).astype(jnp.int32)
    empty_lo = (TILE * empty_col // ROWS_DEV).astype(jnp.int32)
    empty_hi = ((TILE * (empty_col + 1) - 1) // ROWS_DEV).astype(jnp.int32)
    kept_rows = (N_ROW - (empty_hi - empty_lo + 1)).astype(jnp.int32)
    offset = jax.random.randint(block_key, (), 0, kept_rows).astype(jnp.int32)
    chosen_block = ((empty_hi + 1 + offset) % N_ROW).astype(jnp.int32)
    chosen_tile = jax.random.randint(tile_key, (), 0, TR).astype(jnp.int32)
    return (chosen_block, chosen_tile, empty_col, empty_lo, empty_hi, kept_rows)


def empty_rows(empty_lo, empty_hi):
    row_ids = jnp.arange(N_ROW)
    return (row_ids >= empty_lo) & (row_ids <= empty_hi)


def draw_tiles(key, part):
    chosen_block, chosen_tile, empty_col, empty_lo, empty_hi, kept_rows = layout_pick(key)
    raw_tiles = jax.random.randint(jax.random.fold_in(key, 11), (N_ROW, N_COL, TD, TILE, TILE), 0, 16777213).astype(jnp.int32)
    slab = raw_tiles[chosen_block, :, 0]
    partial_total = jnp.sum(slab[:N_COL - 1], axis=0) % 16777213
    closing = ((16777213 - partial_total) % 16777213).astype(jnp.int32)
    slab = slab.at[N_COL - 1].set(closing)
    raw_tiles = raw_tiles.at[chosen_block, :, 0].set(slab)
    return raw_tiles.astype(jnp.float32)


def draw_tile_index(key, part):
    chosen_block, chosen_tile, empty_col, empty_lo, empty_hi, kept_rows = layout_pick(key)
    cells = TR * TC
    devices_all = N_ROW * N_COL
    base_key = jax.random.fold_in(key, 12)
    list_key, short_key, pick_key = jax.random.split(base_key, 3)
    key_list = jax.random.split(list_key, devices_all)
    scores = jax.vmap(lambda device_key: jax.random.permutation(device_key, cells))(key_list).astype(jnp.int32)
    in_block = jnp.arange(devices_all) // N_COL == chosen_block
    in_row = jnp.arange(cells) // TC == chosen_tile
    pushed = scores + cells * (in_block[:, None] & in_row[None, :]).astype(jnp.int32)
    ordered = jnp.argsort(pushed, axis=1, stable=True)[:, :TD].astype(jnp.int32)
    cancel_cell = (chosen_tile * TC + empty_col).astype(jnp.int32)
    leading = jnp.broadcast_to(cancel_cell, (devices_all, 1)).astype(jnp.int32)
    shifted = jnp.concatenate([leading, ordered[:, :TD - 1]], axis=1)
    cell_ids = jnp.where(in_block[:, None], shifted, ordered)
    middle = 1 + jax.random.permutation(short_key, cells - 2)[:TD - 2]
    special = jnp.concatenate([jnp.array([cells - 1, 0], jnp.int32), middle.astype(jnp.int32)])
    chosen = empty_lo * N_COL + jax.random.randint(pick_key, (), 0, N_COL).astype(jnp.int32)
    picked = jnp.arange(devices_all)[:, None] == chosen
    cell_ids = jnp.where(picked, special[None, :], cell_ids)
    tile_slots = jnp.stack([cell_ids // TC, cell_ids % TC], axis=-1).astype(jnp.int32)
    return tile_slots.reshape(N_ROW, N_COL, TD, 2)


def draw_tile_count(key, part):
    chosen_block, chosen_tile, empty_col, empty_lo, empty_hi, kept_rows = layout_pick(key)
    count_key, pick_key, column_key = jax.random.split(jax.random.fold_in(key, 13), 3)
    device_ids = jnp.arange(N_ROW * N_COL)
    slot_counts = jax.random.randint(count_key, (N_ROW * N_COL,), 1, TD + 1)
    busy_row = (empty_hi + 1 + jax.random.randint(pick_key, (), 0, kept_rows).astype(jnp.int32)) % N_ROW
    busiest = busy_row * N_COL + jax.random.randint(column_key, (), 0, N_COL).astype(jnp.int32)
    slot_counts = jnp.where(device_ids == busiest, TD, slot_counts)
    silent_rows = empty_rows(empty_lo, empty_hi)
    slot_counts = jnp.where(silent_rows[device_ids // N_COL], 0, slot_counts)
    return slot_counts.reshape(N_ROW, N_COL).astype(jnp.int32)


def draw_iterate(key, part):
    return draw_residues(jax.random.fold_in(key, 14), (ORDER, BW))


def draw_basis(key, part):
    chosen_block, chosen_tile, empty_col, empty_lo, empty_hi, kept_rows = layout_pick(key)
    fresh = draw_residues(jax.random.fold_in(key, 15), (ORDER, BW)).reshape(N_ROW, N_COL, ROWS_DEV, BW)
    repeated = jnp.broadcast_to(fresh[:, :1], fresh.shape)
    late_rows = empty_rows(empty_lo, empty_hi)[:, None, None, None]
    shaped = jnp.where(late_rows, repeated, fresh).reshape(ORDER, BW)
    row_ids = jnp.arange(ORDER)
    first_row = chosen_block * (ROWS_DEV * N_COL) + chosen_tile * TILE
    silent = (row_ids >= first_row) & (row_ids < first_row + TILE)
    return jnp.where(silent[:, None], jnp.float32(0.0), shaped).astype(jnp.float32)


def draw_coefficients(key, part):
    return draw_residues(jax.random.fold_in(key, 16), (DEG, BW, BW))


def setup_inputs(seed: int = 0) -> dict:
    splits = jax.random.split(jax.random.key(seed), 8)
    return {
        "tiles": draw_tiles(jax.random.fold_in(splits[7], 71), 0),
        "tile_index": draw_tile_index(jax.random.fold_in(splits[7], 71), 0),
        "tile_count": draw_tile_count(jax.random.fold_in(splits[7], 71), 0),
        "iterate": draw_iterate(jax.random.fold_in(splits[7], 71), 0),
        "basis": draw_basis(jax.random.fold_in(splits[7], 71), 0),
        "coefficients": draw_coefficients(jax.random.fold_in(splits[7], 71), 0),
        "start_degree": jax.random.randint(splits[6], (1,), STEPS - 1, DEG).astype(jnp.int32),
    }


PRIME = 16777213
RADIX = 16777216


def fold_word(value):
    value = value % RADIX + 3 * (value // RADIX)
    return jnp.where(value >= PRIME, value - PRIME, value)


def add_mod(first, second):
    total = first + second
    return jnp.where(total >= PRIME, total - PRIME, total)


def shift_mod(value, shift):
    while shift > 0:
        amount = min(shift, 7)
        value = fold_word(value * (2 ** amount))
        shift = shift - amount
    return value


def split_limbs(values, bits, count):
    whole = values.astype(jnp.int32)
    return [((whole // (2 ** (bits * place))) % (2 ** bits)).astype(jnp.bfloat16) for place in range(count)]


def combine_limbs(product, left_bits, right_bits, width):
    whole = product.astype(jnp.int32)
    total = None
    for left in range(whole.shape[-3]):
        for right in range(whole.shape[-1] // width):
            piece = whole[..., left, :, right * width:(right + 1) * width]
            term = shift_mod(piece, left_bits * left + right_bits * right)
            total = term if total is None else add_mod(total, term)
    return total


def reference(tiles, tile_index, tile_count, iterate, basis, coefficients, start_degree):
    basis_limbs = jnp.stack(split_limbs(basis, 8, 3)).astype(jnp.float32)
    current = iterate
    for step in range(STEPS):
        coef = lax.dynamic_index_in_dim(coefficients, start_degree[0] - step, 0, keepdims=False)
        coef_limbs = jnp.concatenate(split_limbs(coef, 8, 3), axis=1).astype(jnp.float32)
        grouped = current.reshape(N_ROW, N_COL, ROWS_DEV, BW).transpose(1, 0, 2, 3).reshape(N_COL, N_ROW * ROWS_DEV, BW)
        column_limbs = jnp.concatenate(split_limbs(grouped, 6, 4), axis=2).astype(jnp.float32)

        def one_block(row_id):
            block = tiles[row_id]
            tile_limbs = jnp.stack(split_limbs(block, 8, 3), axis=2).astype(jnp.float32)
            slots_here = tile_index[row_id]

            def windows_of(limb_rows, column_ids):
                return jax.vmap(lambda column: lax.dynamic_slice_in_dim(limb_rows, column * TILE, TILE, 0))(column_ids)

            windows = jax.vmap(windows_of)(column_limbs, slots_here[:, :, 1])
            product = jnp.einsum("jtlik,jtkc->jtlic", tile_limbs, windows, precision=lax.Precision.HIGHEST)
            residues = combine_limbs(product, 8, 6, BW)
            used = jnp.arange(TD)[None, :] < tile_count[row_id][:, None]
            kept = jnp.where(used[:, :, None, None], residues, 0)
            match = slots_here[:, :, 0][:, :, None] == jnp.arange(TR)[None, None, :]
            partial_value = jnp.sum(jnp.where(match[:, :, :, None, None], kept[:, :, None], 0), axis=(0, 1)) % PRIME
            return partial_value.reshape(TR * TILE, BW)

        products = lax.map(one_block, jnp.arange(N_ROW))
        local = products.reshape(ORDER, BW)
        basis_term = combine_limbs(jnp.einsum("lrk,kc->lrc", basis_limbs, coef_limbs, precision=lax.Precision.HIGHEST), 8, 8, BW)
        current = add_mod(local, basis_term).astype(jnp.float32)
    return current / PRIME
```

```python
import jax
import jax.numpy as jnp
from jax import lax
from jax.experimental import pallas as pl
from jax.experimental.pallas import tpu as pltpu
from jax.sharding import Mesh, PartitionSpec as P

STEPS = 2
PRIME = 16777213
HALF = (PRIME - 1) // 2

ROW = ("zh", "x", "core")
COL = ("zl", "y")

ROUND_16 = 1.5 * 2.0**39
ROUND_8 = 1.5 * 2.0**31

VMEM = pl.BlockSpec(memory_space=pltpu.VMEM)
SMEM = pl.BlockSpec(memory_space=pltpu.SMEM)


def limbs(value):
    high = (value + ROUND_16) - ROUND_16
    rest = value - high
    middle = (rest + ROUND_8) - ROUND_8
    low = rest - middle
    return low.astype(jnp.bfloat16), middle.astype(jnp.bfloat16), high.astype(jnp.bfloat16)


def fold(value):
    return (value & 0xFFFFFF) + 3 * (value >> 24)


def times_256(value):
    return ((value & 0xFFFF) << 8) + 3 * (value >> 16)


def canonical(value):
    value = fold(value)
    value = jnp.where(value < 0, value + PRIME, value)
    return jnp.where(value >= PRIME, value - PRIME, value)


def limb_products(left, right, dims):
    rows = left.shape[0] // 3
    terms = {}
    for place, limb in enumerate(right):
        scaled = left * jnp.bfloat16(2.0 ** (-8 * place))
        product = lax.dot_general(scaled, limb, dims, preferred_element_type=jnp.float32)
        product = product.astype(jnp.int32)
        for other in range(3):
            piece = product[other * rows : (other + 1) * rows]
            weight = place + other
            if weight >= 3:
                weight, piece = weight - 3, 3 * piece
            terms[weight] = terms[weight] + piece if weight in terms else piece
    value = times_256(terms[2]) + terms[1]
    return times_256(value) + terms[0]


def stack_limbs(value, axis):
    low, middle, high = limbs(value)
    return jnp.concatenate(
        [low, middle * jnp.bfloat16(2.0**-8), high * jnp.bfloat16(2.0**-16)], axis=axis
    )


def pack_kernel(degree_ref, place_ref, iterate_ref, coef_ref, out_ref):
    width = iterate_ref.shape[0]
    per_device = coef_ref.shape[0]
    out_ref[:width] = iterate_ref[...]
    parts = []
    for step in range(STEPS):
        wanted = degree_ref[0] - step
        mine = wanted // per_device == place_ref[0]
        coef = jnp.where(mine, coef_ref[wanted % per_device], 0.0)
        parts.extend(coef[8 * q : 8 * q + 8] for q in range(width // 8))
    out_ref[width:] = jnp.concatenate(parts, axis=1)


def tile_kernel(sizes, index_ref, count_ref, core_ref, tile_ref, mine_ref, other_ref, out_ref, total_ref):
    slot = pl.program_id(0)
    pieces, width, half = total_ref.shape
    size_zh, size_x = sizes
    kept = size_zh * size_x * width

    @pl.when(slot == 0)
    def _():
        total_ref[...] = jnp.zeros_like(total_ref)

    @pl.when(slot < count_ref[0])
    def _():
        row = index_ref[2 * slot]
        column = index_ref[2 * slot + 1]
        start = ((column % size_x) * size_zh + column // size_x) * width
        start = pl.multiple_of(start, width)
        mine = mine_ref[pl.ds(start, width), :]
        other = other_ref[pl.ds(start, width), :]
        first = core_ref[0] == 0
        window = jnp.concatenate(
            [jnp.where(first, mine, other), jnp.where(first, other, mine)], axis=1
        )
        window = jnp.where(window > HALF, window - PRIME, window)
        value = limb_products(
            stack_limbs(window, 0), limbs(tile_ref[0]), (((1,), (1,)), ((), ()))
        )
        value = fold(value)
        total_ref[2 * row] += value[:, :half]
        total_ref[2 * row + 1] += value[:, half:]

    @pl.when(slot == pl.num_programs(0) - 1)
    def _():
        value = canonical(total_ref[...]).astype(jnp.float32)
        out_ref[:, :width, :] = value
        if out_ref.shape[1] > width:
            coef = mine_ref[kept:] + other_ref[kept:]
            out_ref[:, width:, :] = jnp.broadcast_to(coef[None], (pieces, *coef.shape))


def finish_kernel(last, received_ref, basis_ref, coef_ref, out_ref, *coef_out_ref):
    sources = received_ref.shape[0]
    width, rows = basis_ref.shape
    total = received_ref[0, :width].astype(jnp.int32)
    for source in range(1, sources):
        total += received_ref[source, :width].astype(jnp.int32)
    if last:
        packed = coef_ref[...]
    else:
        packed = received_ref[0, width:]
        for source in range(1, sources):
            packed += received_ref[source, width:]
        coef_out_ref[0][...] = packed
    first = (STEPS - 1 if last else 0) * (width // 8)
    coef = jnp.concatenate(
        [packed[:, (first + q) * width : (first + q + 1) * width] for q in range(width // 8)], axis=0
    )
    basis_term = limb_products(
        stack_limbs(coef.T, 0), limbs(basis_ref[...]), (((1,), (0,)), ((), ()))
    )
    value = canonical(total + fold(basis_term)).astype(jnp.float32)
    out_ref[...] = value / PRIME if last else value


def gather_row(block, width):
    held = block
    kept = width
    for axis in ("zh", "x"):
        parts = lax.all_gather(held, axis, axis=0, tiled=False)
        data = parts[:, :kept].reshape(-1, parts.shape[-1])
        if parts.shape[1] > kept:
            held = jnp.concatenate([data, parts[:, kept:].sum(0)], axis=0)
        else:
            held = data
        kept = data.shape[0]
    return held, lax.ppermute(held, "core", [(0, 1), (1, 0)])


def tile_products(tiles, index, count, core, mine, other, sizes, width, pieces):
    slots, tile = tiles.shape[0], tiles.shape[1]
    rows_dev = mine.shape[1]
    extra = mine.shape[0] - sizes[0] * sizes[1] * width
    return pl.pallas_call(
        lambda *refs: tile_kernel(sizes, *refs),
        grid=(slots,),
        in_specs=[
            SMEM,
            SMEM,
            SMEM,
            pl.BlockSpec((1, tile, tile), lambda slot: (slot, 0, 0)),
            VMEM,
            VMEM,
        ],
        out_specs=VMEM,
        out_shape=jax.ShapeDtypeStruct((pieces, width + extra, rows_dev), jnp.float32),
        scratch_shapes=[pltpu.VMEM((pieces, width, rows_dev), jnp.int32)],
        compiler_params=pltpu.CompilerParams(vmem_limit_bytes=32 * 1024 * 1024),
    )(index, count, core, tiles, mine, other)


def on_device(tiles, tile_index, tile_count, iterate, basis, coefficients, start_degree):
    block = tiles[0, 0]
    rows_dev, width = iterate.shape
    pieces = lax.axis_size("zl") * lax.axis_size("y")
    index = tile_index[0, 0].reshape(-1)
    count = tile_count[0]
    sizes = lax.axis_size("zh"), lax.axis_size("x")
    core = lax.axis_index("core").astype(jnp.int32).reshape(1)
    place = lax.axis_index((*ROW, *COL)).astype(jnp.int32).reshape(1)
    basis_t = basis.T
    state = jax.ShapeDtypeStruct((width, rows_dev), jnp.float32)
    packed_coef = jax.ShapeDtypeStruct((8, rows_dev), jnp.float32)

    current = pl.pallas_call(
        pack_kernel,
        in_specs=[SMEM, SMEM, VMEM, VMEM],
        out_specs=VMEM,
        out_shape=jax.ShapeDtypeStruct((width + 8, rows_dev), jnp.float32),
    )(start_degree, place, iterate.T, coefficients)
    coef = None
    for step in range(STEPS):
        last = step == STEPS - 1
        mine, other = gather_row(current, width)
        partial = tile_products(block, index, count, core, mine, other, sizes, width, pieces)
        received = lax.all_to_all(partial, COL, 0, 0, tiled=True)
        if last:
            current = pl.pallas_call(
                lambda *refs: finish_kernel(True, *refs),
                in_specs=[VMEM] * 3,
                out_specs=VMEM,
                out_shape=state,
            )(received, basis_t, coef)
        else:
            current, coef = pl.pallas_call(
                lambda received_ref, basis_ref, *outs: finish_kernel(
                    False, received_ref, basis_ref, None, *outs
                ),
                in_specs=[VMEM] * 2,
                out_specs=[VMEM, VMEM],
                out_shape=[state, packed_coef],
            )(received, basis_t)
    return current.T


def solution(mesh):
    parts = Mesh(mesh.devices.reshape(4, 4, 2, 4, 4), (*ROW, *COL))
    in_specs = (
        P(ROW, COL, None, None, None),
        P(ROW, COL, None, None),
        P(ROW, COL),
        P((*ROW, *COL), None),
        P((*ROW, *COL), None),
        P((*ROW, *COL), None, None),
        P(),
    )
    out_specs = P((*ROW, *COL), None)
    return jax.shard_map(
        on_device, mesh=parts, in_specs=in_specs, out_specs=out_specs, check_vma=False
    )
```

```python
import jax
import jax.numpy as jnp
from jax import lax
from jax.experimental import pallas as pl
from jax.experimental.pallas import tpu as pltpu
from jax.sharding import Mesh, PartitionSpec as P

STEPS = 2
PRIME = 16777213
HALF = (PRIME - 1) // 2

ROW = ("zh", "x", "core")
COL = ("zl", "y")

ROUND_16 = 1.5 * 2.0**39
ROUND_8 = 1.5 * 2.0**31

VMEM = pl.BlockSpec(memory_space=pltpu.VMEM)
SMEM = pl.BlockSpec(memory_space=pltpu.SMEM)


def limbs(value):
    high = (value + ROUND_16) - ROUND_16
    rest = value - high
    middle = (rest + ROUND_8) - ROUND_8
    low = rest - middle
    return low.astype(jnp.bfloat16), middle.astype(jnp.bfloat16), high.astype(jnp.bfloat16)


def fold(value):
    return (value & 0xFFFFFF) + 3 * (value >> 24)


def times_256(value):
    return ((value & 0xFFFF) << 8) + 3 * (value >> 16)


def canonical(value):
    value = fold(value)
    value = jnp.where(value < 0, value + PRIME, value)
    return jnp.where(value >= PRIME, value - PRIME, value)


def limb_products(left, right, dims):
    rows = left.shape[0] // 3
    terms = {}
    for place, limb in enumerate(right):
        scaled = left * jnp.bfloat16(2.0 ** (-8 * place))
        product = lax.dot_general(scaled, limb, dims, preferred_element_type=jnp.float32)
        product = product.astype(jnp.int32)
        for other in range(3):
            piece = product[other * rows : (other + 1) * rows]
            weight = place + other
            if weight >= 3:
                weight, piece = weight - 3, 3 * piece
            terms[weight] = terms[weight] + piece if weight in terms else piece
    value = times_256(terms[2]) + terms[1]
    return times_256(value) + terms[0]


def stack_limbs(value, axis):
    low, middle, high = limbs(value)
    return jnp.concatenate(
        [low, middle * jnp.bfloat16(2.0**-8), high * jnp.bfloat16(2.0**-16)], axis=axis
    )


def pack_kernel(degree_ref, place_ref, iterate_ref, coef_ref, out_ref):
    width = iterate_ref.shape[0]
    per_device = coef_ref.shape[0]
    out_ref[:width] = iterate_ref[...]
    parts = []
    for step in range(STEPS):
        wanted = degree_ref[0] - step
        mine = wanted // per_device == place_ref[0]
        coef = jnp.where(mine, coef_ref[wanted % per_device], 0.0)
        parts.extend(coef[8 * q : 8 * q + 8] for q in range(width // 8))
    out_ref[width:] = jnp.concatenate(parts, axis=1)


def split_kernel(tile_ref, after_ref, limb_ref):
    slot = pl.program_id(0)
    for place, limb in enumerate(limbs(tile_ref[0])):
        limb_ref[slot, place] = limb


def tile_kernel(sizes, spread, index_ref, count_ref, core_ref, limb_ref, mine_ref, other_ref, out_ref, total_ref):
    pieces, width, half = total_ref.shape
    size_zh, size_x = sizes
    kept = size_zh * size_x * width
    total_ref[...] = jnp.zeros_like(total_ref)
    for slot in range(limb_ref.shape[0]):

        @pl.when(slot < count_ref[0])
        def _(slot=slot):
            row = index_ref[2 * slot]
            column = index_ref[2 * slot + 1]
            start = ((column % size_x) * size_zh + column // size_x) * width
            start = pl.multiple_of(start, width)
            mine = mine_ref[pl.ds(start, width), :]
            other = other_ref[pl.ds(start, width), :]
            first = core_ref[0] == 0
            window = jnp.concatenate(
                [jnp.where(first, mine, other), jnp.where(first, other, mine)], axis=1
            )
            window = jnp.where(window > HALF, window - PRIME, window)
            value = limb_products(
                stack_limbs(window, 0),
                [limb_ref[slot, place] for place in range(3)],
                (((1,), (1,)), ((), ())),
            )
            value = fold(value)
            total_ref[2 * row] += value[:, :half]
            total_ref[2 * row + 1] += value[:, half:]

    value = canonical(total_ref[...]).astype(jnp.float32)
    if spread is None:
        out_ref[...] = value
    else:
        size_zl, size_y = spread
        for piece in range(pieces):
            at = piece // size_y * width
            out_ref[piece % size_y, at : at + width, :] = value[piece]
        coef = mine_ref[kept:] + other_ref[kept:]
        out_ref[:, size_zl * width :, :] = jnp.broadcast_to(coef[None], (size_y, *coef.shape))


def finish_kernel(last, received_ref, basis_ref, coef_ref, out_ref, *coef_out_ref):
    sources = received_ref.shape[0]
    width, rows = basis_ref.shape
    total = received_ref[0, :width].astype(jnp.int32)
    for source in range(1, sources):
        total += received_ref[source, :width].astype(jnp.int32)
    if last:
        packed = coef_ref[...]
    else:
        packed = received_ref[0, width:]
        for source in range(1, sources):
            packed += received_ref[source, width:]
        coef_out_ref[0][...] = packed
    first = (STEPS - 1 if last else 0) * (width // 8)
    coef = jnp.concatenate(
        [packed[:, (first + q) * width : (first + q + 1) * width] for q in range(width // 8)], axis=0
    )
    basis_term = limb_products(
        stack_limbs(coef.T, 0), limbs(basis_ref[...]), (((1,), (0,)), ((), ()))
    )
    value = canonical(total + fold(basis_term)).astype(jnp.float32)
    out_ref[...] = value / PRIME if last else value


def gather_row(block, width):
    held = block
    kept = width
    for axis in ("zh", "x"):
        if axis == "zh":
            parts = lax.all_gather(held, axis, axis=0, tiled=False)
        else:
            copies = jnp.broadcast_to(held[None], (lax.axis_size(axis), *held.shape))
            parts = lax.all_to_all(copies, axis, 0, 0, tiled=True)
        data = parts[:, :kept].reshape(-1, parts.shape[-1])
        if parts.shape[1] > kept:
            held = jnp.concatenate([data, parts[:, kept:].sum(0)], axis=0)
        else:
            held = data
        kept = data.shape[0]
    return held, lax.ppermute(held, "core", [(0, 1), (1, 0)])


def scatter_col(partial, width):
    received = lax.all_to_all(partial, "y", 0, 0, tiled=True)
    size_zl = lax.axis_size("zl")
    kept = size_zl * width
    value = canonical(received[:, :kept].astype(jnp.int32).sum(0)).astype(jnp.float32)
    value = value.reshape(size_zl, width, -1)
    coef = received[:, kept:].sum(0)
    coef = jnp.broadcast_to(coef[None], (size_zl, *coef.shape))
    return lax.all_to_all(jnp.concatenate([value, coef], axis=1), "zl", 0, 0, tiled=True)


def in_vmem(value):
    return pltpu.with_memory_space_constraint(value, pltpu.VMEM)


def split_tiles(tiles, after):
    slots, tile = tiles.shape[0], tiles.shape[1]
    return pl.pallas_call(
        split_kernel,
        grid=(slots,),
        in_specs=[
            pl.BlockSpec((1, tile, tile), lambda slot: (slot, 0, 0)),
            pl.BlockSpec(memory_space=pl.ANY),
        ],
        out_specs=VMEM,
        out_shape=pltpu.VMEM((slots, 3, tile, tile), jnp.bfloat16),
        compiler_params=pltpu.CompilerParams(vmem_limit_bytes=24 * 1024 * 1024),
        cost_estimate=pl.CostEstimate(
            flops=10 * tiles.size, bytes_accessed=4 * tiles.size, transcendentals=0
        ),
    )(pltpu.with_memory_space_constraint(tiles, pltpu.HBM), after)


def tile_products(tile_limbs, index, count, core, mine, other, sizes, spread, width, pieces):
    rows_dev = mine.shape[1]
    extra = mine.shape[0] - sizes[0] * sizes[1] * width
    if spread is None:
        shape = pieces, width, rows_dev
    else:
        shape = spread[1], spread[0] * width + extra, rows_dev
    return pl.pallas_call(
        lambda *refs: tile_kernel(sizes, spread, *refs),
        in_specs=[SMEM, SMEM, SMEM, VMEM, VMEM, VMEM],
        out_specs=VMEM,
        out_shape=pltpu.VMEM(shape, jnp.float32),
        scratch_shapes=[pltpu.VMEM((pieces, width, rows_dev), jnp.int32)],
        compiler_params=pltpu.CompilerParams(vmem_limit_bytes=24 * 1024 * 1024),
    )(index, count, core, in_vmem(tile_limbs), in_vmem(mine), in_vmem(other))


def on_device(tiles, tile_index, tile_count, iterate, basis, coefficients, start_degree):
    block = tiles[0, 0]
    rows_dev, width = iterate.shape
    spread = lax.axis_size("zl"), lax.axis_size("y")
    pieces = spread[0] * spread[1]
    index = tile_index[0, 0].reshape(-1)
    count = tile_count[0]
    sizes = lax.axis_size("zh"), lax.axis_size("x")
    core = lax.axis_index("core").astype(jnp.int32).reshape(1)
    place = lax.axis_index((*ROW, *COL)).astype(jnp.int32).reshape(1)
    basis_t = basis.T

    current = pl.pallas_call(
        pack_kernel,
        in_specs=[SMEM, SMEM, VMEM, VMEM],
        out_specs=VMEM,
        out_shape=pltpu.VMEM((width + 8, rows_dev), jnp.float32),
    )(start_degree, place, iterate.T, coefficients)
    coef = None
    for step in range(STEPS):
        last = step == STEPS - 1
        mine, other = gather_row(current, width)
        if step == 0:
            tile_limbs = split_tiles(block, mine)
        partial = tile_products(
            tile_limbs, index, count, core, mine, other, sizes, None if last else spread, width, pieces
        )
        if last:
            received = lax.all_to_all(partial, COL, 0, 0, tiled=True)
            current = pl.pallas_call(
                lambda *refs: finish_kernel(True, *refs),
                in_specs=[VMEM] * 3,
                out_specs=VMEM,
                out_shape=jax.ShapeDtypeStruct((width, rows_dev), jnp.float32),
            )(in_vmem(received), basis_t, coef)
        else:
            received = scatter_col(partial, width)
            current, coef = pl.pallas_call(
                lambda received_ref, basis_ref, *outs: finish_kernel(
                    False, received_ref, basis_ref, None, *outs
                ),
                in_specs=[VMEM] * 2,
                out_specs=[VMEM, VMEM],
                out_shape=[
                    pltpu.VMEM((width, rows_dev), jnp.float32),
                    pltpu.VMEM((8, rows_dev), jnp.float32),
                ],
            )(in_vmem(received), basis_t)
    return current.T


def solution(mesh):
    parts = Mesh(mesh.devices.reshape(4, 4, 2, 4, 4), (*ROW, *COL))
    in_specs = (
        P(ROW, COL, None, None, None),
        P(ROW, COL, None, None),
        P(ROW, COL),
        P((*ROW, *COL), None),
        P((*ROW, *COL), None),
        P((*ROW, *COL), None, None),
        P(),
    )
    out_specs = P((*ROW, *COL), None)
    return jax.shard_map(
        on_device, mesh=parts, in_specs=in_specs, out_specs=out_specs, check_vma=False
    )
```

```python
import jax
import jax.numpy as jnp
from jax import lax
from jax.experimental import pallas as pl
from jax.experimental.pallas import tpu as pltpu
from jax.sharding import Mesh, PartitionSpec as P

STEPS = 2
PRIME = 16777213
HALF = (PRIME - 1) // 2

ROW = ("zh", "x", "core")
COL = ("zl", "y")

ROUND_16 = 1.5 * 2.0**39
ROUND_8 = 1.5 * 2.0**31

VMEM = pl.BlockSpec(memory_space=pltpu.VMEM)
SMEM = pl.BlockSpec(memory_space=pltpu.SMEM)


def limbs(value):
    high = (value + ROUND_16) - ROUND_16
    rest = value - high
    middle = (rest + ROUND_8) - ROUND_8
    low = rest - middle
    return low.astype(jnp.bfloat16), middle.astype(jnp.bfloat16), high.astype(jnp.bfloat16)


def fold(value):
    return (value & 0xFFFFFF) + 3 * (value >> 24)


def times_256(value):
    return ((value & 0xFFFF) << 8) + 3 * (value >> 16)


def canonical(value):
    value = fold(value)
    value = jnp.where(value < 0, value + PRIME, value)
    return jnp.where(value >= PRIME, value - PRIME, value)


def limb_products(left, right, dims):
    rows = left.shape[0] // 3
    terms = {}
    for place, limb in enumerate(right):
        scaled = left * jnp.bfloat16(2.0 ** (-8 * place))
        product = lax.dot_general(scaled, limb, dims, preferred_element_type=jnp.float32)
        product = product.astype(jnp.int32)
        for other in range(3):
            piece = product[other * rows : (other + 1) * rows]
            weight = place + other
            if weight >= 3:
                weight, piece = weight - 3, 3 * piece
            terms[weight] = terms[weight] + piece if weight in terms else piece
    value = times_256(terms[2]) + terms[1]
    return times_256(value) + terms[0]


def stack_limbs(value, axis):
    low, middle, high = limbs(value)
    return jnp.concatenate(
        [low, middle * jnp.bfloat16(2.0**-8), high * jnp.bfloat16(2.0**-16)], axis=axis
    )


def pack_kernel(degree_ref, place_ref, iterate_ref, coef_ref, out_ref):
    width = iterate_ref.shape[0]
    per_device = coef_ref.shape[0]
    out_ref[:width] = iterate_ref[...]
    parts = []
    for step in range(STEPS):
        wanted = degree_ref[0] - step
        mine = wanted // per_device == place_ref[0]
        coef = jnp.where(mine, coef_ref[wanted % per_device], 0.0)
        parts.extend(coef[8 * q : 8 * q + 8] for q in range(width // 8))
    out_ref[width:] = jnp.concatenate(parts, axis=1)


def tile_kernel(sizes, spread, half_ref, index_ref, count_ref, tile_ref, gathered_ref, *rest):
    slot = pl.program_id(0)
    size_zh, size_x = sizes
    width = rest[-1].shape[1]
    if spread is None:
        piece_ref, basis_ref, coef_ref = rest[:-1] or (None, None, None)
        total_ref = rest[-1]
    else:
        begun_ref, other_ref, out_ref, total_ref = rest
    half = total_ref.shape[2] // 2

    @pl.when(slot == 0)
    def _():
        if spread is not None:
            total_ref[...] = begun_ref[...]
            return
        total_ref[...] = jnp.zeros_like(total_ref)
        if basis_ref is not None:
            term = fold(basis_product(basis_ref, coef_ref[...], STEPS - 1))
            row = piece_ref[0] // 2
            left = piece_ref[0] % 2 == 0
            total_ref[row, :, :half] = jnp.where(left, term, 0)
            total_ref[row, :, half:] = jnp.where(left, 0, term)

    @pl.when(slot < count_ref[0, 0])
    def _():
        row = index_ref[0, slot]
        column = index_ref[1, slot]
        start = ((column % size_x) * size_zh + column // size_x) * width
        window = gathered_ref[pl.ds(pl.multiple_of(start, width), width), :]
        window = jnp.where(window > HALF, window - PRIME, window)
        value = limb_products(
            stack_limbs(window, 0), limbs(tile_ref[0]), (((1,), (1,)), ((), ()))
        )
        total_ref[row] += fold(value)

    if spread is None:
        return

    @pl.when(slot == pl.num_programs(0) - 1)
    def _():
        value = canonical(total_ref[...]).astype(jnp.float32)
        size_zl, size_y, combined = spread
        kept = size_zh * size_x * width
        for piece in range(size_zl * size_y):
            at = piece % 2 * half
            part = value[piece // 2, :, at : at + half]
            if combined:
                out_ref[piece] = part
            else:
                down = piece // size_y * width
                out_ref[piece % size_y, down : down + width, :] = part
        if not combined:
            coef = gathered_ref[kept:] + other_ref[kept:]
            out_ref[:, size_zl * width :, :] = jnp.broadcast_to(coef[None], (size_y, *coef.shape))


def basis_product(basis_ref, packed, step):
    width = basis_ref.shape[0]
    first = step * (width // 8)
    coef = jnp.concatenate(
        [packed[:, (first + q) * width : (first + q + 1) * width] for q in range(width // 8)], axis=0
    )
    return limb_products(
        stack_limbs(coef.T, 0), limbs(basis_ref[...]), (((1,), (0,)), ((), ()))
    )


def finish_kernel(received_ref, basis_ref, out_ref, coef_ref):
    width = basis_ref.shape[0]
    total = received_ref[0, :width].astype(jnp.int32)
    packed = received_ref[0, width:]
    for source in range(1, received_ref.shape[0]):
        total += received_ref[source, :width].astype(jnp.int32)
        packed += received_ref[source, width:]
    coef_ref[...] = packed
    out_ref[...] = canonical(total + fold(basis_product(basis_ref, packed, 0))).astype(jnp.float32)


def scale_kernel(received_ref, out_ref):
    total = received_ref[0].astype(jnp.int32)
    for source in range(1, received_ref.shape[0]):
        total += received_ref[source].astype(jnp.int32)
    out_ref[...] = canonical(total).astype(jnp.float32) / PRIME


def gather_row(block, width):
    held = block
    kept = width
    for axis in ("zh", "x"):
        if axis == "zh":
            parts = lax.all_gather(held, axis, axis=0, tiled=False)
        else:
            copies = jnp.broadcast_to(held[None], (lax.axis_size(axis), *held.shape))
            parts = lax.all_to_all(copies, axis, 0, 0, tiled=True)
        data = parts[:, :kept].reshape(-1, parts.shape[-1])
        if parts.shape[1] > kept:
            held = jnp.concatenate([data, parts[:, kept:].sum(0)], axis=0)
        else:
            held = data
        kept = data.shape[0]
    return held, lax.ppermute(held, "core", [(0, 1), (1, 0)])


def scatter_col(partial, width):
    received = lax.all_to_all(partial, "y", 0, 0, tiled=True)
    size_zl = lax.axis_size("zl")
    kept = size_zl * width
    value = canonical(received[:, :kept].astype(jnp.int32).sum(0)).astype(jnp.float32)
    value = value.reshape(size_zl, width, -1)
    coef = received[:, kept:].sum(0)
    coef = jnp.broadcast_to(coef[None], (size_zl, *coef.shape))
    return lax.all_to_all(jnp.concatenate([value, coef], axis=1), "zl", 0, 0, tiled=True)


def in_vmem(value):
    return pltpu.with_memory_space_constraint(value, pltpu.VMEM)


def tile_products(tiles, half, index, count, gathered, sizes, width, more, spread=None, shape=None):
    slots, tile = tiles.shape[0], tiles.shape[1]
    rows = sizes[2]
    total = pltpu.VMEM((rows, width, tile), jnp.int32)
    specs = [VMEM if value.ndim > 1 else SMEM for value in more]
    return pl.pallas_call(
        lambda *refs: tile_kernel(sizes[:2], spread, *refs),
        grid_spec=pltpu.PrefetchScalarGridSpec(
            num_scalar_prefetch=3,
            grid=(slots,),
            in_specs=[
                pl.BlockSpec((1, tile, tile // 2), lambda slot, half, *_: (slot, 0, half[0])),
                VMEM,
                *specs,
            ],
            out_specs=VMEM,
            scratch_shapes=[] if spread is None else [total],
        ),
        out_shape=total if spread is None else pltpu.VMEM(shape, jnp.float32),
        compiler_params=pltpu.CompilerParams(vmem_limit_bytes=24 * 1024 * 1024),
        cost_estimate=pl.CostEstimate(
            flops=9 * width * tiles.size, bytes_accessed=2 * tiles.size, transcendentals=0
        ),
    )(
        half,
        index,
        count,
        pltpu.with_memory_space_constraint(tiles, pltpu.HBM),
        in_vmem(gathered),
        *(in_vmem(value) if value.ndim > 1 else value for value in more),
    )


def on_device(tiles, tile_index, tile_count, iterate, basis, coefficients, start_degree):
    block = tiles[0, 0]
    rows_dev, width = iterate.shape
    size_zl, size_y = lax.axis_size("zl"), lax.axis_size("y")
    pieces = size_zl * size_y
    index = tile_index[0, 0].T
    core = lax.axis_index("core").astype(jnp.int32).reshape(1)
    piece = lax.axis_index(COL).astype(jnp.int32).reshape(1)
    place = lax.axis_index((*ROW, *COL)).astype(jnp.int32).reshape(1)
    sizes = lax.axis_size("zh"), lax.axis_size("x"), pieces * rows_dev // block.shape[1]
    basis_t = basis.T

    current = pl.pallas_call(
        pack_kernel,
        in_specs=[SMEM, SMEM, VMEM, VMEM],
        out_specs=VMEM,
        out_shape=pltpu.VMEM((width + 8, rows_dev), jnp.float32),
    )(start_degree, place, iterate.T, coefficients)
    coef = None
    for step in range(STEPS):
        last = step == STEPS - 1
        mine, other = gather_row(current, width)
        total = tile_products(
            block, core, index, tile_count, mine, sizes, width, [piece, basis_t, coef] if last else []
        )
        shape = (pieces, width, rows_dev) if last else (size_y, size_zl * width + 8, rows_dev)
        partial = tile_products(
            block, 1 - core, index, tile_count, other, sizes, width, [total, mine], (size_zl, size_y, last), shape
        )
        if last:
            received = lax.all_to_all(partial, COL, 0, 0, tiled=True)
            current = pl.pallas_call(
                scale_kernel,
                in_specs=[VMEM],
                out_specs=VMEM,
                out_shape=jax.ShapeDtypeStruct((width, rows_dev), jnp.float32),
            )(in_vmem(received))
        else:
            received = scatter_col(partial, width)
            current, coef = pl.pallas_call(
                finish_kernel,
                in_specs=[VMEM] * 2,
                out_specs=[VMEM, VMEM],
                out_shape=[
                    pltpu.VMEM((width, rows_dev), jnp.float32),
                    jax.ShapeDtypeStruct((8, rows_dev), jnp.float32),
                ],
            )(in_vmem(received), basis_t)
    return current.T


def solution(mesh):
    parts = Mesh(mesh.devices.reshape(4, 4, 2, 4, 4), (*ROW, *COL))
    in_specs = (
        P(ROW, COL, None, None, None),
        P(ROW, COL, None, None),
        P(ROW, COL),
        P((*ROW, *COL), None),
        P((*ROW, *COL), None),
        P((*ROW, *COL), None, None),
        P(),
    )
    out_specs = P((*ROW, *COL), None)
    return jax.shard_map(
        on_device, mesh=parts, in_specs=in_specs, out_specs=out_specs, check_vma=False
    )
```

```python
import jax
import jax.numpy as jnp
from jax import lax
from jax.experimental import pallas as pl
from jax.experimental.pallas import tpu as pltpu
from jax.sharding import Mesh, PartitionSpec as P

STEPS = 2
PRIME = 16777213
HALF = (PRIME - 1) // 2

ROW = ("zh", "x", "core")
COL = ("zl", "y")

ROUND_16 = 1.5 * 2.0**39
ROUND_8 = 1.5 * 2.0**31

VMEM = pl.BlockSpec(memory_space=pltpu.VMEM)
SMEM = pl.BlockSpec(memory_space=pltpu.SMEM)


def limbs(value):
    high = (value + ROUND_16) - ROUND_16
    rest = value - high
    middle = (rest + ROUND_8) - ROUND_8
    low = rest - middle
    return low.astype(jnp.bfloat16), middle.astype(jnp.bfloat16), high.astype(jnp.bfloat16)


def fold(value):
    return (value & 0xFFFFFF) + 3 * (value >> 24)


def times_256(value):
    return ((value & 0xFFFF) << 8) + 3 * (value >> 16)


def canonical(value):
    value = fold(value)
    value = jnp.where(value < 0, value + PRIME, value)
    return jnp.where(value >= PRIME, value - PRIME, value)


def limb_products(left, right, dims):
    rows = left.shape[0] // 3
    terms = {}
    for place, limb in enumerate(right):
        scaled = left * jnp.bfloat16(2.0 ** (-8 * place))
        product = lax.dot_general(scaled, limb, dims, preferred_element_type=jnp.float32)
        product = product.astype(jnp.int32)
        for other in range(3):
            piece = product[other * rows : (other + 1) * rows]
            weight = place + other
            if weight >= 3:
                weight, piece = weight - 3, 3 * piece
            terms[weight] = terms[weight] + piece if weight in terms else piece
    value = times_256(terms[2]) + terms[1]
    return times_256(value) + terms[0]


def stack_limbs(value, axis):
    low, middle, high = limbs(value)
    return jnp.concatenate(
        [low, middle * jnp.bfloat16(2.0**-8), high * jnp.bfloat16(2.0**-16)], axis=axis
    )


def pack_kernel(degree_ref, place_ref, iterate_ref, coef_ref, out_ref):
    width = iterate_ref.shape[0]
    per_device = coef_ref.shape[0]
    out_ref[:width] = iterate_ref[...]
    parts = []
    for step in range(STEPS):
        wanted = degree_ref[0] - step
        mine = wanted // per_device == place_ref[0]
        coef = jnp.where(mine, coef_ref[wanted % per_device], 0.0)
        parts.extend(coef[8 * q : 8 * q + 8] for q in range(width // 8))
    out_ref[width:] = jnp.concatenate(parts, axis=1)


def tile_kernel(sizes, spread, half_ref, index_ref, count_ref, *rest):
    size_zh, size_x = sizes
    basis_hbm = None
    if spread is not None:
        tile_hbm, gathered_ref, begun_ref, other_ref, out_ref, total_ref, tile_ref, window_ref, sems = rest
    elif len(rest) == 6:
        tile_hbm, gathered_ref, total_ref, tile_ref, window_ref, sems = rest
    else:
        piece_ref, tile_hbm, gathered_ref, basis_hbm, coef_hbm, *rest = rest
        total_ref, tile_ref, window_ref, sems, basis_ref, coef_ref, extra_sems = rest
    slots, parts, tall, across = tile_ref.shape
    width, half = total_ref.shape[1], total_ref.shape[2] // 2
    left_edge = pl.multiple_of(half_ref[0] * across, across)

    copies = [
        [
            pltpu.make_async_copy(
                tile_hbm.at[slot, pl.ds(part * tall, tall), pl.ds(left_edge, across)],
                tile_ref.at[slot, part],
                sems.at[slot, part],
            )
            for part in range(parts)
        ]
        for slot in range(slots)
    ]
    for copy in sum(copies, []):
        copy.start()
    if basis_hbm is not None:
        extra = [
            pltpu.make_async_copy(basis_hbm, basis_ref, extra_sems.at[0]),
            pltpu.make_async_copy(coef_hbm, coef_ref, extra_sems.at[1]),
        ]
        for copy in extra:
            copy.start()

    for slot in range(slots):

        @pl.when(slot < count_ref[0, 0])
        def _(slot=slot):
            column = index_ref[1, slot]
            start = ((column % size_x) * size_zh + column // size_x) * width
            window = gathered_ref[pl.ds(pl.multiple_of(start, width), width), :]
            window = jnp.where(window > HALF, window - PRIME, window)
            window_ref[slot] = stack_limbs(window, 0)

    total_ref[...] = jnp.zeros_like(total_ref) if spread is None else begun_ref[...]
    if basis_hbm is not None:
        for copy in extra:
            copy.wait()
        term = fold(basis_product(basis_ref, coef_ref[...], STEPS - 1))
        row = piece_ref[0] // 2
        left = piece_ref[0] % 2 == 0
        total_ref[row, :, :half] = jnp.where(left, term, 0)
        total_ref[row, :, half:] = jnp.where(left, 0, term)

    for slot in range(slots):
        for copy in copies[slot]:
            copy.wait()

        @pl.when(slot < count_ref[0, 0])
        def _(slot=slot):
            row = index_ref[0, slot]
            for part in range(parts):
                value = limb_products(
                    window_ref[slot], limbs(tile_ref[slot, part]), (((1,), (1,)), ((), ()))
                )
                total_ref[row, :, part * tall : (part + 1) * tall] += fold(value)

    if spread is None:
        return
    size_zl, size_y, combined = spread
    kept = size_zh * size_x * width
    for row in range(total_ref.shape[0]):
        value = canonical(total_ref[row]).astype(jnp.float32)
        for side in range(2):
            piece = 2 * row + side
            part = value[:, side * half : (side + 1) * half]
            if combined:
                out_ref[piece] = part
            else:
                down = piece // size_y * width
                out_ref[piece % size_y, down : down + width, :] = part
    if not combined:
        coef = gathered_ref[kept:] + other_ref[kept:]
        out_ref[:, size_zl * width :, :] = jnp.broadcast_to(coef[None], (size_y, *coef.shape))


def basis_product(basis_ref, packed, step):
    width = basis_ref.shape[0]
    first = step * (width // 8)
    coef = jnp.concatenate(
        [packed[:, (first + q) * width : (first + q + 1) * width] for q in range(width // 8)], axis=0
    )
    return limb_products(
        stack_limbs(coef.T, 0), limbs(basis_ref[...]), (((1,), (0,)), ((), ()))
    )


def finish_kernel(received_ref, basis_ref, out_ref, coef_ref):
    width = basis_ref.shape[0]
    total = received_ref[0, :width].astype(jnp.int32)
    packed = received_ref[0, width:]
    for source in range(1, received_ref.shape[0]):
        total += received_ref[source, :width].astype(jnp.int32)
        packed += received_ref[source, width:]
    coef_ref[...] = packed
    out_ref[...] = canonical(total + fold(basis_product(basis_ref, packed, 0))).astype(jnp.float32)


def scale_kernel(received_ref, out_ref):
    total = received_ref[0].astype(jnp.int32)
    for source in range(1, received_ref.shape[0]):
        total += received_ref[source].astype(jnp.int32)
    out_ref[...] = canonical(total).astype(jnp.float32) / PRIME


def gather_row(block, width):
    held = block
    kept = width
    for axis in ("zh", "x"):
        if axis == "zh":
            parts = lax.all_gather(held, axis, axis=0, tiled=False)
        else:
            copies = jnp.broadcast_to(held[None], (lax.axis_size(axis), *held.shape))
            parts = lax.all_to_all(copies, axis, 0, 0, tiled=True)
        data = parts[:, :kept].reshape(-1, parts.shape[-1])
        if parts.shape[1] > kept:
            held = jnp.concatenate([data, parts[:, kept:].sum(0)], axis=0)
        else:
            held = data
        kept = data.shape[0]
    return held, lax.ppermute(held, "core", [(0, 1), (1, 0)])


def scatter_col(partial, width):
    received = lax.all_to_all(partial, "y", 0, 0, tiled=True)
    size_zl = lax.axis_size("zl")
    kept = size_zl * width
    value = canonical(received[:, :kept].astype(jnp.int32).sum(0)).astype(jnp.float32)
    value = value.reshape(size_zl, width, -1)
    coef = received[:, kept:].sum(0)
    coef = jnp.broadcast_to(coef[None], (size_zl, *coef.shape))
    return lax.all_to_all(jnp.concatenate([value, coef], axis=1), "zl", 0, 0, tiled=True)


def in_vmem(value):
    return pltpu.with_memory_space_constraint(value, pltpu.VMEM)


def tile_products(tiles, half, index, count, gathered, sizes, width, basis=None, spread=None, shape=None, more=()):
    slots, tile = tiles.shape[0], tiles.shape[1]
    parts = 2
    total = pltpu.VMEM((sizes[2], width, tile), jnp.int32)
    scratch = [
        pltpu.VMEM((slots, parts, tile // parts, tile // 2), jnp.float32),
        pltpu.VMEM((slots, 3 * width, tile // 2), jnp.bfloat16),
        pltpu.SemaphoreType.DMA((slots, parts)),
    ]
    scalars, fetched = [half, index, count], []
    if basis is not None:
        scalars, fetched = [*scalars, basis[0]], list(basis[1:])
        scratch += [pltpu.VMEM(value.shape, value.dtype) for value in fetched]
        scratch += [pltpu.SemaphoreType.DMA((len(fetched),))]
    hbm = pl.BlockSpec(memory_space=pl.ANY)
    return pl.pallas_call(
        lambda *refs: tile_kernel(sizes[:2], spread, *refs),
        in_specs=[SMEM] * len(scalars) + [hbm, VMEM] + [hbm] * len(fetched) + [VMEM] * len(more),
        out_specs=VMEM,
        out_shape=total if spread is None else pltpu.VMEM(shape, jnp.float32),
        scratch_shapes=scratch if spread is None else [total, *scratch],
        compiler_params=pltpu.CompilerParams(vmem_limit_bytes=24 * 1024 * 1024),
        cost_estimate=pl.CostEstimate(
            flops=9 * width * tiles.size, bytes_accessed=2 * tiles.size, transcendentals=0
        ),
    )(
        *scalars,
        pltpu.with_memory_space_constraint(tiles, pltpu.HBM),
        in_vmem(gathered),
        *fetched,
        *(in_vmem(value) for value in more),
    )


def on_device(tiles, tile_index, tile_count, iterate, basis, coefficients, start_degree):
    block = tiles[0, 0]
    rows_dev, width = iterate.shape
    size_zl, size_y = lax.axis_size("zl"), lax.axis_size("y")
    pieces = size_zl * size_y
    index = tile_index[0, 0].T
    core = lax.axis_index("core").astype(jnp.int32).reshape(1)
    piece = lax.axis_index(COL).astype(jnp.int32).reshape(1)
    place = lax.axis_index((*ROW, *COL)).astype(jnp.int32).reshape(1)
    sizes = lax.axis_size("zh"), lax.axis_size("x"), pieces * rows_dev // block.shape[1]
    basis_t = basis.T

    current = pl.pallas_call(
        pack_kernel,
        in_specs=[SMEM, SMEM, VMEM, VMEM],
        out_specs=VMEM,
        out_shape=pltpu.VMEM((width + 8, rows_dev), jnp.float32),
    )(start_degree, place, iterate.T, coefficients)
    coef = None
    for step in range(STEPS):
        last = step == STEPS - 1
        mine, other = gather_row(current, width)
        total = tile_products(
            block, core, index, tile_count, mine, sizes, width, (piece, basis_t, coef) if last else None
        )
        shape = (pieces, width, rows_dev) if last else (size_y, size_zl * width + 8, rows_dev)
        partial = tile_products(
            block, 1 - core, index, tile_count, other, sizes, width, None, (size_zl, size_y, last), shape, (total, mine)
        )
        if last:
            received = lax.all_to_all(partial, COL, 0, 0, tiled=True)
            current = pl.pallas_call(
                scale_kernel,
                in_specs=[VMEM],
                out_specs=VMEM,
                out_shape=jax.ShapeDtypeStruct((width, rows_dev), jnp.float32),
            )(in_vmem(received))
        else:
            received = scatter_col(partial, width)
            current, coef = pl.pallas_call(
                finish_kernel,
                in_specs=[VMEM] * 2,
                out_specs=[VMEM, VMEM],
                out_shape=[
                    pltpu.VMEM((width, rows_dev), jnp.float32),
                    pltpu.VMEM((8, rows_dev), jnp.float32),
                ],
            )(in_vmem(received), basis_t)
    return current.T


def solution(mesh):
    parts = Mesh(mesh.devices.reshape(4, 4, 2, 4, 4), (*ROW, *COL))
    in_specs = (
        P(ROW, COL, None, None, None),
        P(ROW, COL, None, None),
        P(ROW, COL),
        P((*ROW, *COL), None),
        P((*ROW, *COL), None),
        P((*ROW, *COL), None, None),
        P(),
    )
    out_specs = P((*ROW, *COL), None)
    return jax.shard_map(
        on_device, mesh=parts, in_specs=in_specs, out_specs=out_specs, check_vma=False
    )
```

```python
import jax
import jax.numpy as jnp
from jax import lax
from jax.experimental import pallas as pl
from jax.experimental.pallas import tpu as pltpu
from jax.sharding import Mesh, PartitionSpec as P

STEPS = 2
PRIME = 16777213
HALF = (PRIME - 1) // 2

ROW = ("zh", "x", "core")
COL = ("zl", "y")

ROUND_16 = 1.5 * 2.0**39
ROUND_8 = 1.5 * 2.0**31

VMEM = pl.BlockSpec(memory_space=pltpu.VMEM)
SMEM = pl.BlockSpec(memory_space=pltpu.SMEM)


def limbs(value):
    high = (value + ROUND_16) - ROUND_16
    rest = value - high
    middle = (rest + ROUND_8) - ROUND_8
    low = rest - middle
    return low.astype(jnp.bfloat16), middle.astype(jnp.bfloat16), high.astype(jnp.bfloat16)


def fold(value):
    return (value & 0xFFFFFF) + 3 * (value >> 24)


def times_256(value):
    return ((value & 0xFFFF) << 8) + 3 * (value >> 16)


def canonical(value):
    value = fold(value)
    value = jnp.where(value < 0, value + PRIME, value)
    return jnp.where(value >= PRIME, value - PRIME, value)


def limb_products(left, right, dims):
    rows = left.shape[0] // 3
    terms = {}
    for place, limb in enumerate(right):
        scaled = left * jnp.bfloat16(2.0 ** (-8 * place))
        product = lax.dot_general(scaled, limb, dims, preferred_element_type=jnp.float32)
        product = product.astype(jnp.int32)
        for other in range(3):
            piece = product[other * rows : (other + 1) * rows]
            weight = place + other
            if weight >= 3:
                weight, piece = weight - 3, 3 * piece
            terms[weight] = terms[weight] + piece if weight in terms else piece
    value = times_256(terms[2]) + terms[1]
    return times_256(value) + terms[0]


def stack_limbs(value, axis):
    low, middle, high = limbs(value)
    return jnp.concatenate(
        [low, middle * jnp.bfloat16(2.0**-8), high * jnp.bfloat16(2.0**-16)], axis=axis
    )


def pack_kernel(degree_ref, place_ref, iterate_ref, coef_ref, out_ref):
    width = iterate_ref.shape[0]
    per_device = coef_ref.shape[0]
    out_ref[:width] = iterate_ref[...]
    parts = []
    for step in range(STEPS):
        wanted = degree_ref[0] - step
        mine = wanted // per_device == place_ref[0]
        coef = jnp.where(mine, coef_ref[wanted % per_device], 0.0)
        parts.extend(coef[8 * q : 8 * q + 8] for q in range(width // 8))
    out_ref[width:] = jnp.concatenate(parts, axis=1)


def tile_kernel(sizes, spread, half_ref, index_ref, count_ref, *rest):
    size_zh, size_x = sizes
    basis_hbm = None
    fetched = []
    if spread is not None:
        tile_ref, gathered_ref, begun_ref, other_ref, out_ref, total_ref, window_ref = rest
    elif len(rest) == 4:
        tile_ref, gathered_ref, total_ref, window_ref = rest
    else:
        piece_ref, tile_hbm, gathered_ref, basis_hbm, coef_hbm, *rest = rest
        total_ref, later_ref, tile_ref, window_ref, sems, basis_ref, coef_ref, extra_sems = rest
    slots, parts, tall, across = tile_ref.shape
    width, half = total_ref.shape[1], total_ref.shape[2] // 2
    columns = pl.ds(pl.multiple_of(half_ref[0] * half, half) if across > half else 0, half)

    if basis_hbm is not None:
        for turn, target in enumerate((tile_ref, later_ref)):
            edge = jnp.where(turn == 0, half_ref[0], 1 - half_ref[0]) * across
            fetched.append(
                [
                    pltpu.make_async_copy(
                        tile_hbm.at[slot, pl.ds(part * tall, tall), pl.ds(pl.multiple_of(edge, across), across)],
                        target.at[slot, part],
                        sems.at[turn, slot, part],
                    )
                    for slot in range(slots)
                    for part in range(parts)
                ]
            )
        for copy in fetched[0]:
            copy.start()
        extra = [
            pltpu.make_async_copy(basis_hbm, basis_ref, extra_sems.at[0]),
            pltpu.make_async_copy(coef_hbm, coef_ref, extra_sems.at[1]),
        ]
        for copy in extra:
            copy.start()
        for copy in fetched[1]:
            copy.start()

    for slot in range(slots):
        column = jnp.where(slot < count_ref[0, 0], index_ref[1, slot], 0)
        start = ((column % size_x) * size_zh + column // size_x) * width
        window = gathered_ref[pl.ds(pl.multiple_of(start, width), width), :]
        window = jnp.where(window > HALF, window - PRIME, window)
        window_ref[slot] = stack_limbs(window, 0)

    total_ref[...] = jnp.zeros_like(total_ref) if spread is None else begun_ref[...]
    if basis_hbm is not None:
        for copy in extra:
            copy.wait()
        term = fold(basis_product(basis_ref, coef_ref[...], STEPS - 1))
        row = piece_ref[0] // 2
        left = piece_ref[0] % 2 == 0
        total_ref[row, :, :half] = jnp.where(left, term, 0)
        total_ref[row, :, half:] = jnp.where(left, 0, term)

    for slot in range(slots):
        if fetched and slot % 2 == 0:
            for copy in fetched[0][slot * parts : (slot + 2) * parts]:
                copy.wait()

        used = slot < count_ref[0, 0]
        row = jnp.where(used, index_ref[0, slot], 0)
        for part in range(parts):
            value = limb_products(
                window_ref[slot], limbs(tile_ref[slot, part, :, columns]), (((1,), (1,)), ((), ()))
            )
            total_ref[row, :, part * tall : (part + 1) * tall] += jnp.where(used, fold(value), 0)

    if fetched:
        for copy in fetched[1]:
            copy.wait()
    if spread is None:
        return
    size_zl, size_y, combined = spread
    kept = size_zh * size_x * width
    for row in range(total_ref.shape[0]):
        value = canonical(total_ref[row]).astype(jnp.float32)
        for side in range(2):
            piece = 2 * row + side
            part = value[:, side * half : (side + 1) * half]
            if combined:
                out_ref[piece] = part
            else:
                down = piece // size_y * width
                out_ref[piece % size_y, down : down + width, :] = part
    if not combined:
        coef = gathered_ref[kept:] + other_ref[kept:]
        out_ref[:, size_zl * width :, :] = jnp.broadcast_to(coef[None], (size_y, *coef.shape))


def basis_product(basis_ref, packed, step):
    width = basis_ref.shape[0]
    first = step * (width // 8)
    coef = jnp.concatenate(
        [packed[:, (first + q) * width : (first + q + 1) * width] for q in range(width // 8)], axis=0
    )
    return limb_products(
        stack_limbs(coef.T, 0), limbs(basis_ref[...]), (((1,), (0,)), ((), ()))
    )


def finish_kernel(received_ref, basis_ref, out_ref, coef_ref):
    width = basis_ref.shape[0]
    total = received_ref[0, :width].astype(jnp.int32)
    packed = received_ref[0, width:]
    for source in range(1, received_ref.shape[0]):
        total += received_ref[source, :width].astype(jnp.int32)
        packed += received_ref[source, width:]
    coef_ref[...] = packed
    out_ref[...] = canonical(total + fold(basis_product(basis_ref, packed, 0))).astype(jnp.float32)


def scale_kernel(received_ref, out_ref):
    total = received_ref[0].astype(jnp.int32)
    for source in range(1, received_ref.shape[0]):
        total += received_ref[source].astype(jnp.int32)
    out_ref[...] = canonical(total).astype(jnp.float32) / PRIME


def gather_row(block, width):
    held = block
    kept = width
    for axis in ("zh", "x"):
        if axis == "zh":
            parts = lax.all_gather(held, axis, axis=0, tiled=False)
        else:
            copies = jnp.broadcast_to(held[None], (lax.axis_size(axis), *held.shape))
            parts = lax.all_to_all(copies, axis, 0, 0, tiled=True)
        data = parts[:, :kept].reshape(-1, parts.shape[-1])
        if parts.shape[1] > kept:
            held = jnp.concatenate([data, parts[:, kept:].sum(0)], axis=0)
        else:
            held = data
        kept = data.shape[0]
    return held, lax.ppermute(held, "core", [(0, 1), (1, 0)])


def scatter_col(partial, width):
    received = lax.all_to_all(partial, "y", 0, 0, tiled=True)
    size_zl = lax.axis_size("zl")
    kept = size_zl * width
    value = canonical(received[:, :kept].astype(jnp.int32).sum(0)).astype(jnp.float32)
    value = value.reshape(size_zl, width, -1)
    coef = received[:, kept:].sum(0)
    coef = jnp.broadcast_to(coef[None], (size_zl, *coef.shape))
    return lax.all_to_all(jnp.concatenate([value, coef], axis=1), "zl", 0, 0, tiled=True)


def in_vmem(value):
    return pltpu.with_memory_space_constraint(value, pltpu.VMEM)


def tile_start(tiles, half, index, count, gathered, sizes, width, basis=None):
    slots, tile = tiles.shape[0], tiles.shape[1]
    parts = 2
    blocks = tiles.reshape(slots, parts, tile // parts, tile)
    total = pltpu.VMEM((sizes[2], width, tile), jnp.int32)
    windows = pltpu.VMEM((slots, 3 * width, tile // 2), jnp.bfloat16)
    params = pltpu.CompilerParams(vmem_limit_bytes=24 * 1024 * 1024)
    cost = pl.CostEstimate(flops=9 * width * tiles.size, bytes_accessed=4 * tiles.size, transcendentals=0)
    if basis is None:
        begun = pl.pallas_call(
            lambda *refs: tile_kernel(sizes[:2], None, *refs),
            in_specs=[SMEM] * 3 + [VMEM] * 2,
            out_specs=VMEM,
            out_shape=total,
            scratch_shapes=[windows],
            compiler_params=params,
            cost_estimate=cost,
        )(half, index, count, blocks, in_vmem(gathered))
        return begun, blocks
    halves = pltpu.VMEM((slots, parts, tile // parts, tile // 2), jnp.float32)
    fetched = basis[1:]
    hbm = pl.BlockSpec(memory_space=pl.ANY)
    return pl.pallas_call(
        lambda *refs: tile_kernel(sizes[:2], None, *refs),
        in_specs=[SMEM] * 4 + [hbm, VMEM] + [hbm] * len(fetched),
        out_specs=[VMEM, VMEM],
        out_shape=[total, halves],
        scratch_shapes=[
            halves,
            windows,
            pltpu.SemaphoreType.DMA((2, slots, parts)),
            *[pltpu.VMEM(value.shape, value.dtype) for value in fetched],
            pltpu.SemaphoreType.DMA((len(fetched),)),
        ],
        compiler_params=params,
        cost_estimate=cost,
    )(
        half,
        index,
        count,
        basis[0],
        pltpu.with_memory_space_constraint(tiles, pltpu.HBM),
        in_vmem(gathered),
        *fetched,
    )


def tile_end(halves, total, half, index, count, gathered, other, sizes, width, spread, shape):
    slots, tile = halves.shape[0], total.shape[2]
    return pl.pallas_call(
        lambda *refs: tile_kernel(sizes[:2], spread, *refs),
        in_specs=[SMEM] * 3 + [VMEM] * 4,
        out_specs=VMEM,
        out_shape=pltpu.VMEM(shape, jnp.float32),
        scratch_shapes=[
            pltpu.VMEM(total.shape, jnp.int32),
            pltpu.VMEM((slots, 3 * width, tile // 2), jnp.bfloat16),
        ],
        compiler_params=pltpu.CompilerParams(vmem_limit_bytes=24 * 1024 * 1024),
    )(half, index, count, halves, *(in_vmem(value) for value in (gathered, total, other)))


def on_device(tiles, tile_index, tile_count, iterate, basis, coefficients, start_degree):
    block = tiles[0, 0]
    rows_dev, width = iterate.shape
    size_zl, size_y = lax.axis_size("zl"), lax.axis_size("y")
    pieces = size_zl * size_y
    index = tile_index[0, 0].T
    core = lax.axis_index("core").astype(jnp.int32).reshape(1)
    piece = lax.axis_index(COL).astype(jnp.int32).reshape(1)
    place = lax.axis_index((*ROW, *COL)).astype(jnp.int32).reshape(1)
    sizes = lax.axis_size("zh"), lax.axis_size("x"), pieces * rows_dev // block.shape[1]
    basis_t = basis.T

    current = pl.pallas_call(
        pack_kernel,
        in_specs=[SMEM, SMEM, VMEM, VMEM],
        out_specs=VMEM,
        out_shape=pltpu.VMEM((width + 8, rows_dev), jnp.float32),
    )(start_degree, place, iterate.T, coefficients)
    coef = None
    for step in range(STEPS):
        last = step == STEPS - 1
        mine, other = gather_row(current, width)
        total, halves = tile_start(
            block, core, index, tile_count, mine, sizes, width, (piece, basis_t, coef) if last else None
        )
        shape = (pieces, width, rows_dev) if last else (size_y, size_zl * width + 8, rows_dev)
        partial = tile_end(
            halves, total, 1 - core, index, tile_count, other, mine, sizes, width, (size_zl, size_y, last), shape
        )
        if last:
            received = lax.all_to_all(partial, COL, 0, 0, tiled=True)
            current = pl.pallas_call(
                scale_kernel,
                in_specs=[VMEM],
                out_specs=VMEM,
                out_shape=jax.ShapeDtypeStruct((width, rows_dev), jnp.float32),
            )(in_vmem(received))
        else:
            received = scatter_col(partial, width)
            current, coef = pl.pallas_call(
                finish_kernel,
                in_specs=[VMEM] * 2,
                out_specs=[VMEM, VMEM],
                out_shape=[
                    pltpu.VMEM((width, rows_dev), jnp.float32),
                    pltpu.VMEM((8, rows_dev), jnp.float32),
                ],
            )(in_vmem(received), basis_t)
    return current.T


def solution(mesh):
    parts = Mesh(mesh.devices.reshape(4, 4, 2, 4, 4), (*ROW, *COL))
    in_specs = (
        P(ROW, COL, None, None, None),
        P(ROW, COL, None, None),
        P(ROW, COL),
        P((*ROW, *COL), None),
        P((*ROW, *COL), None),
        P((*ROW, *COL), None, None),
        P(),
    )
    out_specs = P((*ROW, *COL), None)
    return jax.shard_map(
        on_device, mesh=parts, in_specs=in_specs, out_specs=out_specs, check_vma=False
    )
```

```python
import jax
import jax.numpy as jnp
from jax import lax
from jax.experimental import pallas as pl
from jax.experimental.pallas import tpu as pltpu
from jax.sharding import Mesh, PartitionSpec as P

STEPS = 2
PRIME = 16777213
HALF = (PRIME - 1) // 2

ROW = ("zh", "x", "core")
COL = ("zl", "y")

ROUND_16 = 1.5 * 2.0**39
ROUND_8 = 1.5 * 2.0**31

VMEM = pl.BlockSpec(memory_space=pltpu.VMEM)
SMEM = pl.BlockSpec(memory_space=pltpu.SMEM)


def limbs(value):
    high = (value + ROUND_16) - ROUND_16
    rest = value - high
    middle = (rest + ROUND_8) - ROUND_8
    low = rest - middle
    return low.astype(jnp.bfloat16), middle.astype(jnp.bfloat16), high.astype(jnp.bfloat16)


def fold(value):
    return (value & 0xFFFFFF) + 3 * (value >> 24)


def times_256(value):
    return ((value & 0xFFFF) << 8) + 3 * (value >> 16)


def canonical(value):
    value = fold(value)
    value = jnp.where(value < 0, value + PRIME, value)
    return jnp.where(value >= PRIME, value - PRIME, value)


def limb_products(left, right, dims):
    rows = left.shape[0] // 3
    terms = {}
    for place, limb in enumerate(right):
        scaled = left * jnp.bfloat16(2.0 ** (-8 * place))
        product = lax.dot_general(scaled, limb, dims, preferred_element_type=jnp.float32)
        product = product.astype(jnp.int32)
        for other in range(3):
            piece = product[other * rows : (other + 1) * rows]
            weight = place + other
            if weight >= 3:
                weight, piece = weight - 3, 3 * piece
            terms[weight] = terms[weight] + piece if weight in terms else piece
    value = times_256(terms[2]) + terms[1]
    return times_256(value) + terms[0]


def stack_limbs(value, axis):
    low, middle, high = limbs(value)
    return jnp.concatenate(
        [low, middle * jnp.bfloat16(2.0**-8), high * jnp.bfloat16(2.0**-16)], axis=axis
    )


def pack_kernel(degree_ref, place_ref, iterate_ref, coef_ref, out_ref):
    width = iterate_ref.shape[0]
    per_device = coef_ref.shape[0]
    out_ref[:width] = iterate_ref[...]
    parts = []
    for step in range(STEPS):
        wanted = degree_ref[0] - step
        mine = wanted // per_device == place_ref[0]
        coef = jnp.where(mine, coef_ref[wanted % per_device], 0.0)
        parts.extend(coef[8 * q : 8 * q + 8] for q in range(width // 8))
    out_ref[width:] = jnp.concatenate(parts, axis=1)


def tile_kernel(sizes, spread, half_ref, index_ref, count_ref, *rest):
    size_zh, size_x = sizes
    basis_hbm = None
    fetched = []
    if spread is not None:
        tile_ref, gathered_ref, begun_ref, other_ref, out_ref, total_ref, window_ref = rest
    elif len(rest) == 4:
        tile_ref, gathered_ref, total_ref, window_ref = rest
    else:
        piece_ref, tile_hbm, gathered_ref, basis_hbm, coef_hbm, *rest = rest
        total_ref, later_ref, tile_ref, window_ref, sems, basis_ref, coef_ref, extra_sems = rest
    slots, parts, tall, across = tile_ref.shape
    width, half = total_ref.shape[1], total_ref.shape[2] // 2

    def side(slot):
        column = jnp.where(slot < count_ref[0, 0], index_ref[1, slot], 0)
        return (half_ref[0] + column // size_x) % 2

    if basis_hbm is not None:
        for turn, target in enumerate((tile_ref, later_ref)):
            edges = [pl.multiple_of((side(slot) + turn) % 2 * across, across) for slot in range(slots)]
            fetched.append(
                [
                    pltpu.make_async_copy(
                        tile_hbm.at[slot, pl.ds(part * tall, tall), pl.ds(edges[slot], across)],
                        target.at[slot, part],
                        sems.at[turn, slot, part],
                    )
                    for slot in range(slots)
                    for part in range(parts)
                ]
            )
        for copy in fetched[0]:
            copy.start()
        extra = [
            pltpu.make_async_copy(basis_hbm, basis_ref, extra_sems.at[0]),
            pltpu.make_async_copy(coef_hbm, coef_ref, extra_sems.at[1]),
        ]
        for copy in extra:
            copy.start()
        for copy in fetched[1]:
            copy.start()

    for slot in range(slots):
        column = jnp.where(slot < count_ref[0, 0], index_ref[1, slot], 0)
        start = ((column % size_x) * size_zh + column // size_x) * width
        window = gathered_ref[pl.ds(pl.multiple_of(start, width), width), :]
        window = jnp.where(window > HALF, window - PRIME, window)
        window_ref[slot] = stack_limbs(window, 0)

    total_ref[...] = jnp.zeros_like(total_ref) if spread is None else begun_ref[...]
    if basis_hbm is not None:
        for copy in extra:
            copy.wait()
        term = fold(basis_product(basis_ref, coef_ref[...], STEPS - 1))
        row = piece_ref[0] // 2
        left = piece_ref[0] % 2 == 0
        total_ref[row, :, :half] = jnp.where(left, term, 0)
        total_ref[row, :, half:] = jnp.where(left, 0, term)

    for slot in range(slots):
        if fetched and slot % 2 == 0:
            for copy in fetched[0][slot * parts : (slot + 2) * parts]:
                copy.wait()

        used = slot < count_ref[0, 0]
        row = jnp.where(used, index_ref[0, slot], 0)
        columns = pl.ds(pl.multiple_of(side(slot) * half, half) if across > half else 0, half)
        for part in range(parts):
            value = limb_products(
                window_ref[slot], limbs(tile_ref[slot, part, :, columns]), (((1,), (1,)), ((), ()))
            )
            total_ref[row, :, part * tall : (part + 1) * tall] += jnp.where(used, fold(value), 0)

    if fetched:
        for copy in fetched[1]:
            copy.wait()
    if spread is None:
        return
    size_zl, size_y, combined = spread
    kept = size_zh * size_x * width
    for row in range(total_ref.shape[0]):
        value = canonical(total_ref[row]).astype(jnp.float32)
        for side in range(2):
            piece = 2 * row + side
            part = value[:, side * half : (side + 1) * half]
            if combined:
                out_ref[piece] = part
            else:
                down = piece // size_y * width
                out_ref[piece % size_y, down : down + width, :] = part
    if not combined:
        coef = gathered_ref[kept:] + other_ref[kept:]
        out_ref[:, size_zl * width :, :] = jnp.broadcast_to(coef[None], (size_y, *coef.shape))


def basis_product(basis_ref, packed, step):
    width = basis_ref.shape[0]
    first = step * (width // 8)
    coef = jnp.concatenate(
        [packed[:, (first + q) * width : (first + q + 1) * width] for q in range(width // 8)], axis=0
    )
    return limb_products(
        stack_limbs(coef.T, 0), limbs(basis_ref[...]), (((1,), (0,)), ((), ()))
    )


def finish_kernel(received_ref, basis_ref, out_ref, coef_ref):
    width = basis_ref.shape[0]
    total = received_ref[0, :width].astype(jnp.int32)
    packed = received_ref[0, width:]
    for source in range(1, received_ref.shape[0]):
        total += received_ref[source, :width].astype(jnp.int32)
        packed += received_ref[source, width:]
    coef_ref[...] = packed
    out_ref[...] = canonical(total + fold(basis_product(basis_ref, packed, 0))).astype(jnp.float32)


def scale_kernel(received_ref, out_ref):
    total = received_ref[0].astype(jnp.int32)
    for source in range(1, received_ref.shape[0]):
        total += received_ref[source].astype(jnp.int32)
    out_ref[...] = canonical(total).astype(jnp.float32) / PRIME


def gather_row(block, width):
    held = block
    kept = width
    for axis in ("zh", "x"):
        if axis == "zh":
            groups = [[2 * at + (at + first) % 2 for at in range(lax.axis_size(axis))] for first in range(2)]
            parts = lax.all_gather(held, (axis, "core"), axis=0, tiled=False, axis_index_groups=groups)
        else:
            copies = jnp.broadcast_to(held[None], (lax.axis_size(axis), *held.shape))
            parts = lax.all_to_all(copies, axis, 0, 0, tiled=True)
        data = parts[:, :kept].reshape(-1, parts.shape[-1])
        if parts.shape[1] > kept:
            held = jnp.concatenate([data, parts[:, kept:].sum(0)], axis=0)
        else:
            held = data
        kept = data.shape[0]
    return held, lax.ppermute(held, "core", [(0, 1), (1, 0)])


def scatter_col(partial, width):
    received = lax.all_to_all(partial, "y", 0, 0, tiled=True)
    size_zl = lax.axis_size("zl")
    kept = size_zl * width
    value = canonical(received[:, :kept].astype(jnp.int32).sum(0)).astype(jnp.float32)
    value = value.reshape(size_zl, width, -1)
    coef = received[:, kept:].sum(0)
    coef = jnp.broadcast_to(coef[None], (size_zl, *coef.shape))
    return lax.all_to_all(jnp.concatenate([value, coef], axis=1), "zl", 0, 0, tiled=True)


def in_vmem(value):
    return pltpu.with_memory_space_constraint(value, pltpu.VMEM)


def tile_start(tiles, half, index, count, gathered, sizes, width, basis=None):
    slots, tile = tiles.shape[0], tiles.shape[1]
    parts = 2
    blocks = tiles.reshape(slots, parts, tile // parts, tile)
    total = pltpu.VMEM((sizes[2], width, tile), jnp.int32)
    windows = pltpu.VMEM((slots, 3 * width, tile // 2), jnp.bfloat16)
    params = pltpu.CompilerParams(vmem_limit_bytes=24 * 1024 * 1024)
    cost = pl.CostEstimate(flops=9 * width * tiles.size, bytes_accessed=4 * tiles.size, transcendentals=0)
    if basis is None:
        begun = pl.pallas_call(
            lambda *refs: tile_kernel(sizes[:2], None, *refs),
            in_specs=[SMEM] * 3 + [VMEM] * 2,
            out_specs=VMEM,
            out_shape=total,
            scratch_shapes=[windows],
            compiler_params=params,
            cost_estimate=cost,
        )(half, index, count, blocks, in_vmem(gathered))
        return begun, blocks
    halves = pltpu.VMEM((slots, parts, tile // parts, tile // 2), jnp.float32)
    fetched = basis[1:]
    hbm = pl.BlockSpec(memory_space=pl.ANY)
    return pl.pallas_call(
        lambda *refs: tile_kernel(sizes[:2], None, *refs),
        in_specs=[SMEM] * 4 + [hbm, VMEM] + [hbm] * len(fetched),
        out_specs=[VMEM, VMEM],
        out_shape=[total, halves],
        scratch_shapes=[
            halves,
            windows,
            pltpu.SemaphoreType.DMA((2, slots, parts)),
            *[pltpu.VMEM(value.shape, value.dtype) for value in fetched],
            pltpu.SemaphoreType.DMA((len(fetched),)),
        ],
        compiler_params=params,
        cost_estimate=cost,
    )(
        half,
        index,
        count,
        basis[0],
        pltpu.with_memory_space_constraint(tiles, pltpu.HBM),
        in_vmem(gathered),
        *fetched,
    )


def tile_end(halves, total, half, index, count, gathered, other, sizes, width, spread, shape):
    slots, tile = halves.shape[0], total.shape[2]
    return pl.pallas_call(
        lambda *refs: tile_kernel(sizes[:2], spread, *refs),
        in_specs=[SMEM] * 3 + [VMEM] * 4,
        out_specs=VMEM,
        out_shape=pltpu.VMEM(shape, jnp.float32),
        scratch_shapes=[
            pltpu.VMEM(total.shape, jnp.int32),
            pltpu.VMEM((slots, 3 * width, tile // 2), jnp.bfloat16),
        ],
        compiler_params=pltpu.CompilerParams(vmem_limit_bytes=24 * 1024 * 1024),
    )(half, index, count, halves, *(in_vmem(value) for value in (gathered, total, other)))


def on_device(tiles, tile_index, tile_count, iterate, basis, coefficients, start_degree):
    block = tiles[0, 0]
    rows_dev, width = iterate.shape
    size_zl, size_y = lax.axis_size("zl"), lax.axis_size("y")
    pieces = size_zl * size_y
    index = tile_index[0, 0].T
    half = ((lax.axis_index("core") + lax.axis_index("zh")) % 2).astype(jnp.int32).reshape(1)
    piece = lax.axis_index(COL).astype(jnp.int32).reshape(1)
    place = lax.axis_index((*ROW, *COL)).astype(jnp.int32).reshape(1)
    sizes = lax.axis_size("zh"), lax.axis_size("x"), pieces * rows_dev // block.shape[1]
    basis_t = basis.T

    current = pl.pallas_call(
        pack_kernel,
        in_specs=[SMEM, SMEM, VMEM, VMEM],
        out_specs=VMEM,
        out_shape=pltpu.VMEM((width + 8, rows_dev), jnp.float32),
    )(start_degree, place, iterate.T, coefficients)
    coef = None
    for step in range(STEPS):
        last = step == STEPS - 1
        mine, other = gather_row(current, width)
        total, halves = tile_start(
            block, half, index, tile_count, mine, sizes, width, (piece, basis_t, coef) if last else None
        )
        shape = (pieces, width, rows_dev) if last else (size_y, size_zl * width + 8, rows_dev)
        partial = tile_end(
            halves, total, 1 - half, index, tile_count, other, mine, sizes, width, (size_zl, size_y, last), shape
        )
        if last:
            received = lax.all_to_all(partial, COL, 0, 0, tiled=True)
            current = pl.pallas_call(
                scale_kernel,
                in_specs=[VMEM],
                out_specs=VMEM,
                out_shape=jax.ShapeDtypeStruct((width, rows_dev), jnp.float32),
            )(in_vmem(received))
        else:
            received = scatter_col(partial, width)
            current, coef = pl.pallas_call(
                finish_kernel,
                in_specs=[VMEM] * 2,
                out_specs=[VMEM, VMEM],
                out_shape=[
                    pltpu.VMEM((width, rows_dev), jnp.float32),
                    pltpu.VMEM((8, rows_dev), jnp.float32),
                ],
            )(in_vmem(received), basis_t)
    return current.T


def solution(mesh):
    parts = Mesh(mesh.devices.reshape(4, 4, 2, 4, 4), (*ROW, *COL))
    in_specs = (
        P(ROW, COL, None, None, None),
        P(ROW, COL, None, None),
        P(ROW, COL),
        P((*ROW, *COL), None),
        P((*ROW, *COL), None),
        P((*ROW, *COL), None, None),
        P(),
    )
    out_specs = P((*ROW, *COL), None)
    return jax.shard_map(
        on_device, mesh=parts, in_specs=in_specs, out_specs=out_specs, check_vma=False
    )
```
